32 devices in a mesh: groups: 2 (over y), head: 2 (over x), tok: 4 (over z), sub: 2 (over core).
Axes of the slice: x: 2, y: 2, z: 4, core: 2. Of those that a mesh axis runs over, the one named last changes fastest.
Arguments:
- prefill_query: bfloat16 [4096, 128, 192], P(('groups', 'tok'), ('head', 'sub')), parts along dimension 0, may hold values from -60 to 60
- prefill_latent: bfloat16 [8, 512, 512], P(('groups', 'tok'), ('head', 'sub')), parts along dimension 0, may hold values from -6 to 6
- prefill_rope: bfloat16 [8, 512, 64], P(('groups', 'tok'), ('head', 'sub')), parts along dimension 0, may hold values from -6 to 6
- span_blocks: int32 [16], P('groups'), parts along dimension 0, may hold values from 1 to 16, 32 in all
- span_pad: int32 [16], P('groups'), parts along dimension 0, may hold values from 0 to 63
- key_weight: bfloat16 [128, 512, 128], P(('head', 'sub')), may hold values from -0.25 to 0.25
- value_weight: bfloat16 [128, 512, 128], P(('head', 'sub')), may hold values from -0.25 to 0.25
- decode_query: bfloat16 [64, 128, 2, 288], P(('groups', 'tok'), 'head', 'sub'), parts along dimension 0, may hold values from -60 to 60
- decode_cache: bfloat16 [64, 256, 2, 288], P(('groups', 'tok'), 'head', 'sub'), parts along dimension 0, may hold values from -6 to 6
- decode_lengths: int32 [64], P(('groups', 'tok')), parts along dimension 0, may hold values from 1 to 256, 4096 in all
- decode_pages: int32 [64, 8], P(('groups', 'tok'), 'head'), parts along dimension 0, may hold values from 0 to 7, each once within a row
Outputs:
- prefill_out: bfloat16 [4096, 128, 128], P(('groups', 'tok'), ('head', 'sub')), parts along dimension 0
- decode_context: bfloat16 [64, 128, 2, 256], P(('groups', 'tok'), 'head', 'sub'), parts along dimension 0
The draws below stay inside these ranges and needn't reach their ends.
There are 2 independent parts, one for each index of `groups`. The reference program is written for one: setup_inputs(seed, part) draws one part's arguments, and reference() takes and returns one part's arrays. A program takes and returns all parts, laid end to end along the dimension named above; an argument that names none is the same for every part. Nothing has to cross between parts.
Inputs may be any that keep to these rules, and one draw needn't show every extreme that they name: `span_blocks`: sums to 32; the largest entry is exactly 16. `decode_lengths`: some row has exactly 256. `decode_pages`: each row is a permutation of 0 to 7.
All inputs are finite; a program needn't handle non-finite values. No bound on the sum of `decode_lengths` on one device may be relied on, other than what follows from the above.
Results may differ from the reference program's by a relative error of at most 0.0056.
Values may be sent and summed in bfloat16 or wider, within the bound.
No kernel may reach another device: no remote copies, remote signals or barrier semaphores. Data moves between devices by JAX's collectives and lax.ppermute only.
A program may use at most 192 MiB of HBM per device.

```python
import math
import jax
import jax.numpy as jnp
import numpy as np
from jax import lax

H = 128
C = 512
R = 64
DN = 128
DV = 128
TOK_BLOCK = 64
PAGE = 32
PRE_BLOCK = 512
CTX_DEV = 128
PRE_TOK = 2048
NBLK = 32
NCHUNK = 8
MOST_BLOCKS = 16
ROWS_DEC = 32
CTX = 256
NPAGE = 8
N_HEAD = 2
N_TOK = 4


def draw_prefill_rope(key, part):
    key = jax.random.fold_in(key, 11)
    full_shape = (N_TOK, PRE_BLOCK, R)
    result = jax.random.truncated_normal(key, -6.0, 6.0, full_shape, jnp.float32)
    return result.astype(jnp.bfloat16)


def draw_prefill_query(key, part):
    key = jax.random.fold_in(key, 12)
    full_shape = (PRE_TOK, H, DN + R)
    result = jax.random.truncated_normal(key, -6.0, 6.0, full_shape, jnp.float32)
    return result.astype(jnp.bfloat16)


def draw_decode_query(key, part):
    key = jax.random.fold_in(key, 13)
    latent_half = C // 2
    rope_half = R // 2
    full_shape = (ROWS_DEC, H, 2, latent_half + rope_half)
    result = jax.random.truncated_normal(key, -6.0, 6.0, full_shape, jnp.float32)
    return result.astype(jnp.bfloat16)


def draw_decode_cache(key, part):
    key = jax.random.fold_in(key, 14)
    latent_half = C // 2
    rope_half = R // 2
    full_shape = (ROWS_DEC, CTX, 2, latent_half + rope_half)
    result = jax.random.truncated_normal(key, -6.0, 6.0, full_shape, jnp.float32)
    return result.astype(jnp.bfloat16)


def place_ends(values, own_key, smallest, top_value):
    shape = values.shape
    index_at = [jax.random.randint(jax.random.fold_in(own_key, axis), (), 0, shape[axis]) for axis in range(len(shape))]
    values = values.at[tuple(index_at)].set(smallest)
    longest = shape.index(max(shape))
    index_at[longest] = (index_at[longest] + 1) % shape[longest]
    return values.at[tuple(index_at)].set(top_value)


def block_scale(key, extent, pieces, smallest, high):
    level, own = 1.0, jax.random.fold_in(key, 6)
    for dim, shards_of in pieces:
        steps = jnp.exp(jax.random.uniform(jax.random.fold_in(own, dim), (shards_of,), jnp.float32, smallest / len(pieces), high / len(pieces)))
        level = level * jnp.repeat(steps, extent[dim] // shards_of).reshape([-1 if axis == dim else 1 for axis in range(len(extent))])
    return level


def split_up(count, total, most, lean):
    weights = [(1 << 20) // math.isqrt(grade ** lean) + 1 for grade in range(2, count + 1)]
    rest, counts = total - most - (count - 1), [1] * (count - 1)
    while rest > 0:
        free = [i for i in range(count - 1) if counts[i] < most]
        mass, remaining = sum([weights[i] for i in free]), rest
        for i in free:
            more = min(most - counts[i], max(1, remaining * weights[i] // mass), rest)
            counts[i] = counts[i] + more
            rest = rest - more
    return np.array([most] + counts)


def ragged_sizes(key, amount, total, most, lean):
    if amount == 2:
        one = jax.random.randint(key, (), max(1, total - most), min(most, total - 1) + 1)
        return jnp.stack([one, total - one])
    lengths = jnp.asarray(split_up(amount, total, most, lean), jnp.int32)
    couples = (amount - 1) // 2
    source_of, taker = lengths[1:1 + 2 * couples:2], lengths[2:2 + 2 * couples:2]
    margin = jnp.minimum(source_of - 1, most - taker)
    passed = jax.random.randint(jax.random.fold_in(key, 1), (couples,), 0, 1 << 20) % (margin + 1)
    lengths = lengths.at[1:1 + 2 * couples:2].set(source_of - passed).at[2:2 + 2 * couples:2].set(taker + passed)
    return lengths[jax.random.permutation(jax.random.fold_in(key, 2), amount)]


def bell_draw(own_key, dims, width, reach, cuts=(), kind=jnp.bfloat16):
    array = jax.random.normal(own_key, dims, jnp.float32) * width
    if len(cuts) > 0:
        array = block_scale(own_key, dims, cuts, -0.22, 0.18) * array
    return jnp.clip(array, min=-reach, max=reach).astype(kind)


def setup_inputs(seed: int = 0, part: int = 0) -> dict:
    splits = jax.random.split(jax.random.key(seed), 12)
    own_keys = jax.random.split(jax.random.fold_in(splits[11], part), 12)
    return {
        "prefill_query": draw_prefill_query(jax.random.fold_in(jax.random.fold_in(splits[11], part), 71), part),
        "prefill_latent": bell_draw(own_keys[1], (N_TOK, PRE_BLOCK, C), 1.0, 6.0, ((0, 4), (1, 4))),
        "prefill_rope": draw_prefill_rope(jax.random.fold_in(jax.random.fold_in(splits[11], part), 71), part),
        "span_blocks": ragged_sizes(own_keys[3], NCHUNK, NBLK, MOST_BLOCKS, 2).astype(jnp.int32),
        "span_pad": place_ends(jax.random.randint(own_keys[4], (NCHUNK,), 0, TOK_BLOCK), jax.random.fold_in(own_keys[4], 1), 0, TOK_BLOCK - 1).astype(jnp.int32),
        "key_weight": bell_draw(splits[5], (H, C, DN), C ** -0.5, 0.25, ((0, 4),)),
        "value_weight": bell_draw(splits[6], (H, C, DV), C ** -0.5, 0.25, ((0, 4),)),
        "decode_query": draw_decode_query(jax.random.fold_in(jax.random.fold_in(splits[11], part), 71), part),
        "decode_cache": draw_decode_cache(jax.random.fold_in(jax.random.fold_in(splits[11], part), 71), part),
        "decode_lengths": ragged_sizes(own_keys[9], ROWS_DEC, ROWS_DEC * CTX // 2, CTX, 2).astype(jnp.int32),
        "decode_pages": jax.vmap(lambda own: jax.random.permutation(own, NPAGE))(jax.random.split(own_keys[10], ROWS_DEC)).reshape((ROWS_DEC, NPAGE)).astype(jnp.int32),
    }


MASKED_SCORE = -1e+30

def span_limits(span_blocks, span_pad, positions):
    span_ends = (jnp.cumsum(span_blocks) * TOK_BLOCK).astype(jnp.int32)
    span_of = lax.optimization_barrier(jnp.sum((positions[:, None] >= span_ends[None, :]).astype(jnp.int32), axis=1)).astype(jnp.int32)
    onehot = (span_of[:, None] == jnp.arange(span_blocks.shape[0], dtype=jnp.int32)[None, :]).astype(jnp.int32)
    valid_end = lax.optimization_barrier(jnp.sum(onehot * (span_ends - span_pad).astype(jnp.int32)[None, :], axis=1)).astype(jnp.int32)
    return (span_of, valid_end)

def attend(queries, key_rows, value_rows, visible, score_scale):
    scores = jnp.dot(queries, key_rows.T, preferred_element_type=jnp.float32) * score_scale
    scores = jnp.where(visible, scores, MASKED_SCORE)
    row_peak = lax.optimization_barrier(jnp.max(scores, axis=1, keepdims=True))
    weights = jnp.where(visible, jnp.exp(scores - row_peak), 0.0)
    totals = lax.optimization_barrier(jnp.sum(weights, axis=1, keepdims=True))
    blended = jnp.dot(weights.astype(jnp.bfloat16), value_rows, preferred_element_type=jnp.float32)
    return blended / totals

def reference(prefill_query, prefill_latent, prefill_rope, span_blocks, span_pad, key_weight, value_weight, decode_query, decode_cache, decode_lengths, decode_pages):
    score_scale = 1.0 / math.sqrt(DN + R)
    latent = prefill_latent.reshape(PRE_TOK, C)
    rope_rows = prefill_rope.reshape(PRE_TOK, R)
    weight = jnp.concatenate([key_weight, value_weight], axis=2)
    expanded = jnp.einsum('tc,hcd->htd', latent.astype(jnp.float32), weight.astype(jnp.float32)).astype(jnp.bfloat16)
    positions = jnp.arange(PRE_TOK, dtype=jnp.int32)
    span_of, valid_end = span_limits(span_blocks, span_pad, positions)
    visible = (span_of[:, None] == span_of[None, :]) & (positions[None, :] <= positions[:, None]) & (positions < valid_end)[None, :]

    def one_head(pair):
        queries, head_rows = pair
        key_rows = jnp.concatenate([head_rows[:, :DN], rope_rows], axis=1)
        return attend(queries, key_rows, head_rows[:, DN:], visible, score_scale)
    outputs = lax.map(one_head, (jnp.transpose(prefill_query, (1, 0, 2)), expanded))
    outputs = jnp.transpose(outputs, (1, 0, 2))
    prefill_out = jnp.where((positions < valid_end)[:, None, None], outputs, 0.0).astype(jnp.bfloat16)
    slots = jnp.arange(CTX, dtype=jnp.int32)
    logical = decode_pages[:, slots // PAGE] * PAGE + (slots % PAGE)[None, :]
    live_tokens = logical < decode_lengths[:, None]
    latent_half = C // 2

    def one_row(triple):
        row_query, row_cache, row_live = triple
        scores = jnp.einsum('hsc,tsc->ht', row_query.astype(jnp.float32), row_cache.astype(jnp.float32)) * score_scale
        scores = jnp.where(row_live[None, :], scores, MASKED_SCORE).reshape(H, N_HEAD, CTX_DEV)
        live_blocks = row_live.reshape(N_HEAD, CTX_DEV)[None, :, :]
        block_peak = lax.optimization_barrier(jnp.max(scores, axis=2))
        weights = jnp.where(live_blocks, jnp.exp(scores - block_peak[:, :, None]), 0.0)
        block_totals = lax.optimization_barrier(jnp.sum(weights, axis=2))
        blocks_cache = row_cache[:, :, :latent_half].reshape(N_HEAD, CTX_DEV, 2, latent_half).astype(jnp.float32)
        block_context = jnp.einsum('hjt,jtsc->hjsc', weights.astype(jnp.bfloat16).astype(jnp.float32), blocks_cache)
        row_peak = lax.optimization_barrier(jnp.max(block_peak, axis=1, keepdims=True))
        factor = jnp.exp(block_peak - row_peak)
        totals = lax.optimization_barrier(jnp.sum(block_totals * factor, axis=1))
        context = lax.optimization_barrier(jnp.sum(block_context * factor[:, :, None, None], axis=1))
        return (context / totals[:, None, None]).astype(jnp.bfloat16)
    decode_context = lax.map(one_row, (decode_query, decode_cache, live_tokens))
    return (prefill_out, decode_context)
```

```python
import functools
import math

import jax
import jax.numpy as jnp
from jax import lax
from jax.experimental import pallas as pl
from jax.experimental.pallas import tpu as pltpu
from jax.sharding import PartitionSpec as P

C = 512
R = 64
DN = 128
DV = 128
TOK_BLOCK = 64
MOST_BLOCKS = 16
PAGE = 32

MASKED_SCORE = -1e30
LOG2E = math.log2(math.e)

VMEM_LIMIT = 56 * 1024 * 1024
KEY_CHUNK = 256
HEAD_GROUP = 4
HEAD_BLOCK = 16


def prompt_kernel(n_pieces, tok_ref, place_ref, blocks_ref, pad_ref, q_ref, wk_ref, wv_ref, *refs):
    pieces, (o_ref, keys_ref, k_scr, bias_scr, live_scr, out_scr) = refs[:n_pieces], refs[n_pieces:]
    key_chunk = KEY_CHUNK
    group, width, nq = q_ref.shape
    nk = keys_ref.shape[0]
    n_span = blocks_ref.shape[0]
    steps = o_ref.shape[1] // group
    origin = tok_ref[0] * nq - (nk - nq)
    scale = LOG2E / math.sqrt(DN + R)
    step = pl.program_id(0)

    starts, limits = [], []
    end = -origin
    for i in range(n_span):
        starts.append(end)
        end = end + blocks_ref[i] * TOK_BLOCK
        limits.append(end - pad_ref[i])

    def span_of(position):
        first, limit = starts[0], limits[0]
        for i in range(1, n_span):
            inside = position >= starts[i]
            first = jnp.where(inside, starts[i], first)
            limit = jnp.where(inside, limits[i], limit)
        return first, limit

    @pl.when(step == 0)
    def _():
        position = (nk - nq) + lax.broadcasted_iota(jnp.int32, (8, nq), 1)
        first, limit = span_of(position)
        final = jnp.minimum(position, limit - 1)
        live_scr[...] = (position < limit).astype(jnp.float32)
        def fill(i, _):
            key = i * 64 + lax.broadcasted_iota(jnp.int32, (64, nq), 0)
            visible = (key >= first[:1]) & (key <= final[:1])
            bias_scr[pl.ds(pl.multiple_of(i * 64, 64), 64), :] = jnp.where(visible, 0.0, MASKED_SCORE)
            return 0
        lax.fori_loop(0, nk // 64, fill, 0)
        for i, piece in enumerate(pieces):
            rows = pl.ds(pl.multiple_of(place_ref[i], 16), piece.shape[0])
            keys_ref[rows, :] = piece[:, :C]
            for g in range(group):
                k_scr[g, rows, DN:] = piece[:, C:]

    c_first = lax.div(span_of(jnp.int32(nk - nq))[0], key_chunk)

    def run(first):
        rows = slice(first, nk)
        for g in range(group):
            weight = jnp.concatenate([wk_ref[g], wv_ref[g]], axis=1)
            both = jnp.dot(keys_ref[rows, :], weight, preferred_element_type=jnp.float32).astype(jnp.bfloat16)
            k_scr[g, rows, :DN] = both[:, :DN]
            values = both[:, DN:].T
            s = jnp.dot(k_scr[g, rows, :], q_ref[g], preferred_element_type=jnp.float32)
            s = s + bias_scr[rows, :]
            top = jnp.max(s, axis=0, keepdims=True) * scale
            p = jnp.exp2(s * scale - top)
            total = jnp.sum(p, axis=0, keepdims=True)
            out = jnp.dot(values, p.astype(jnp.bfloat16), preferred_element_type=jnp.float32)
            out = out * (live_scr[:1, :] / total)
            slot = lax.rem(step, steps) * group + g
            out_scr[slot, :nq, :] = out.T

    for c in range((nk - nq) // key_chunk + 1):
        @pl.when(c_first == c)
        def _(c=c):
            run(c * key_chunk)

    @pl.when(lax.rem(step, steps) == steps - 1)
    def _():
        heads = o_ref.shape[1]
        stride = out_scr.shape[1]
        flat = out_scr.reshape(heads * stride, DV)
        def move(i, _):
            for u in range(16):
                p = i * 16 + u
                o_ref[p] = flat[pl.ds(p, heads, stride=stride), :].astype(o_ref.dtype)
            return 0
        lax.fori_loop(0, nq // 16, move, 0)


def prompt_attention(tok, places, span_blocks, span_pad, queries, key_weight, value_weight, pieces):
    heads, width, nq = queries.shape
    nk = sum(piece.shape[0] for piece in pieces)
    group = math.gcd(HEAD_GROUP, heads)
    block = math.gcd(HEAD_BLOCK, heads)
    grid_spec = pltpu.PrefetchScalarGridSpec(
        num_scalar_prefetch=4,
        grid=(heads // group,),
        in_specs=[
            pl.BlockSpec((group, width, nq), lambda i, *_: (i, 0, 0)),
            pl.BlockSpec((group, C, DN), lambda i, *_: (i, 0, 0)),
            pl.BlockSpec((group, C, DV), lambda i, *_: (i, 0, 0)),
        ]
        + [pl.BlockSpec(piece.shape, lambda i, *_: (0, 0)) for piece in pieces],
        out_specs=pl.BlockSpec((nq, block, DV), lambda i, *_: (0, i // (block // group), 0)),
        scratch_shapes=[
            pltpu.VMEM((nk, C), jnp.bfloat16),
            pltpu.VMEM((group, nk, width), jnp.bfloat16),
            pltpu.VMEM((nk, nq), jnp.float32),
            pltpu.VMEM((8, nq), jnp.float32),
            pltpu.VMEM((block, nq + 8, DV), jnp.float32),
        ],
    )
    return pl.pallas_call(
        functools.partial(prompt_kernel, len(pieces)),
        out_shape=jax.ShapeDtypeStruct((nq, heads, DV), jnp.bfloat16),
        grid_spec=grid_spec,
        compiler_params=pltpu.CompilerParams(
            dimension_semantics=("arbitrary",), vmem_limit_bytes=VMEM_LIMIT
        ),
        cost_estimate=pl.CostEstimate(
            flops=2 * heads * nk * (C * (DN + DV) + nq * (width + DV)),
            bytes_accessed=24 << 20,
            transcendentals=heads * nq * nk,
        ),
        name="prompt_attention",
    )(tok, places, span_blocks, span_pad, queries, key_weight, value_weight, *pieces)


def decode_kernel(lengths_ref, pages_ref, other_pages_ref, qm_ref, qs_ref, mm_ref, ms_ref, om_ref, os_ref, o_ref):
    rows, width, slots = mm_ref.shape
    half = o_ref.shape[2]
    scale = LOG2E / math.sqrt(DN + R)
    lane = lax.broadcasted_iota(jnp.int32, (1, slots), 1)
    page_of, inside = lax.div(lane, PAGE), lax.rem(lane, PAGE)

    def live(ref, row):
        position = inside + ref[row, 0] * PAGE
        for j in range(1, ref.shape[1]):
            position = jnp.where(page_of == j, inside + ref[row, j] * PAGE, position)
        return position < lengths_ref[row]

    def dot(a, b):
        return jnp.dot(a, b, preferred_element_type=jnp.float32)

    def blend(w, cache):
        return lax.dot_general(
            w.astype(jnp.bfloat16),
            cache,
            (((1,), (1,)), ((), ())),
            preferred_element_type=jnp.float32,
        )

    for row in range(rows):
        qm, qs = qm_ref[row], qs_ref[row]
        near, far = live(pages_ref, row), live(other_pages_ref, row)
        s_near = dot(qm, mm_ref[row]) + dot(qs, ms_ref[row])
        s_far = dot(qm, om_ref[row]) + dot(qs, os_ref[row])
        s_near = jnp.where(near, s_near, MASKED_SCORE)
        s_far = jnp.where(far, s_far, MASKED_SCORE)
        top = jnp.max(jnp.maximum(s_near, s_far), axis=1, keepdims=True) * scale
        w_near = jnp.exp2(s_near * scale - top)
        w_far = jnp.exp2(s_far * scale - top)
        total = jnp.sum(w_near + w_far, axis=1, keepdims=True)
        context = blend(w_near, mm_ref[row, :half, :]) + blend(w_far, om_ref[row, :half, :])
        o_ref[row] = (context / total).astype(o_ref.dtype)


def decode_pair(lengths, pages, other_pages, qm, qs, mm, ms, om, os):
    rows, heads, width = qm.shape
    half = width - R // 2
    smem = pl.BlockSpec(memory_space=pltpu.SMEM)
    vmem = pl.BlockSpec(memory_space=pltpu.VMEM)
    return pl.pallas_call(
        decode_kernel,
        out_shape=jax.ShapeDtypeStruct((rows, heads, half), jnp.bfloat16),
        in_specs=[smem] * 3 + [vmem] * 6,
        out_specs=vmem,
        compiler_params=pltpu.CompilerParams(vmem_limit_bytes=VMEM_LIMIT),
        cost_estimate=pl.CostEstimate(
            flops=8 * rows * heads * mm.shape[2] * (width + half // 2),
            bytes_accessed=4 << 20,
            transcendentals=2 * rows * heads * mm.shape[2],
        ),
        name="decode_pair",
    )(lengths, pages, other_pages, qm, qs, mm, ms, om, os)


def swap(x, axis):
    return lax.ppermute(x, axis, [(0, 1), (1, 0)])


def prompt_pieces(prefill_latent, prefill_rope, sizes):
    n_tok, n_head, n_sub = sizes
    rows = prefill_latent.shape[1]
    block_rows = rows * n_head * n_sub
    back = min(n_tok - 1, -(-(MOST_BLOCKS - 1) * TOK_BLOCK // block_rows))
    own = jnp.concatenate([prefill_latent[0], prefill_rope[0]], axis=1)
    blocks = [own] + [
        lax.ppermute(own, "tok", [(i, i + d) for i in range(n_tok - d)]) for d in range(1, back + 1)
    ]
    if n_head == 2 and n_sub == 2:
        head, sub = lax.axis_index("head"), lax.axis_index("sub")
        pieces, places = [], []
        for d, mine in enumerate(blocks):
            far = swap(mine, "head")
            for h, x in enumerate((mine, far)):
                for s, y in enumerate((x, swap(x, "sub"))):
                    pieces.append(y)
                    index = ((back - d) * n_head + (head ^ h)) * n_sub + (sub ^ s)
                    places.append(index * rows)
        return pieces, jnp.stack(places).astype(jnp.int32)
    keys = jnp.stack(blocks[::-1])
    keys = lax.all_gather(keys, ("head", "sub"), axis=1, tiled=True)
    return [keys.reshape(-1, C + R)], jnp.zeros((1,), jnp.int32)


def decode_exchange(decode_query, decode_cache, decode_lengths, decode_pages):
    score_scale = 1.0 / math.sqrt(DN + R)
    queries_all = lax.all_gather(decode_query, "head", axis=1, tiled=True)
    partial_value = jnp.einsum(
        "bhsc,btsc->bht", queries_all, decode_cache, preferred_element_type=jnp.float32
    )
    scores = lax.psum(partial_value, "sub") * score_scale
    page_count = decode_pages.shape[1]
    logical = (
        jnp.repeat(decode_pages, PAGE, axis=1) * PAGE
        + jnp.tile(jnp.arange(PAGE, dtype=jnp.int32), page_count)[None, :]
    )
    live_tokens = logical < decode_lengths[:, None]
    scores = jnp.where(live_tokens[:, None, :], scores, MASKED_SCORE)
    peak_here = jnp.max(scores, axis=2)
    weights = jnp.where(live_tokens[:, None, :], jnp.exp(scores - peak_here[:, :, None]), 0.0)
    totals = jnp.sum(weights, axis=2)
    latent_half = decode_cache.shape[3] - R // 2
    context = jnp.einsum(
        "bht,btsc->bhsc",
        weights.astype(jnp.bfloat16),
        decode_cache[:, :, :, :latent_half],
        preferred_element_type=jnp.float32,
    )
    peaks_in, totals_in, context_in = (
        lax.all_to_all(peak_here[None], "head", split_axis=2, concat_axis=0, tiled=True),
        lax.all_to_all(totals[None], "head", split_axis=2, concat_axis=0, tiled=True),
        lax.all_to_all(context[None], "head", split_axis=2, concat_axis=0, tiled=True),
    )
    row_peak = jnp.max(peaks_in, axis=0)
    factor = jnp.exp(peaks_in - row_peak[None])
    denominators = jnp.sum(totals_in * factor, axis=0)
    summed = jnp.sum(context_in * factor[:, :, :, None, None], axis=0)
    decode_context = (summed / denominators[:, :, None, None]).astype(jnp.bfloat16)
    return decode_context


def local(
    sizes,
    prefill_query,
    prefill_latent,
    prefill_rope,
    span_blocks,
    span_pad,
    key_weight,
    value_weight,
    decode_query,
    decode_cache,
    decode_lengths,
    decode_pages,
):
    n_head, n_sub = sizes[1:]
    tok = lax.axis_index("tok")
    paired = n_head == 2 and n_sub == 2
    pieces, places = prompt_pieces(prefill_latent, prefill_rope, sizes)
    if paired:
        qm = decode_query[:, :, 0, :]
        mm = jnp.transpose(decode_cache[:, :, 0, :], (0, 2, 1))
        qs, ms = swap(qm, "sub"), swap(mm, "sub")
        mm_out, ms_out, *pieces = lax.optimization_barrier((mm, ms, *pieces))
        om, os = swap(mm_out, "head"), swap(ms_out, "head")
        other_pages = swap(decode_pages, "head")

    prefill_out = prompt_attention(
        tok[None].astype(jnp.int32),
        places,
        span_blocks,
        span_pad,
        jnp.transpose(prefill_query, (1, 2, 0)),
        key_weight,
        value_weight,
        pieces,
    )
    if paired:
        prefill_out, om, os, other_pages = lax.optimization_barrier((prefill_out, om, os, other_pages))
        context = decode_pair(decode_lengths, decode_pages, other_pages, qm, qs, mm, ms, om, os)
        decode_context = context[:, :, None, :]
    else:
        decode_context = decode_exchange(decode_query, decode_cache, decode_lengths, decode_pages)
    return (prefill_out, decode_context)


def solution(mesh):
    in_specs = (
        P(("groups", "tok"), ("head", "sub"), None),
        P(("groups", "tok"), ("head", "sub"), None),
        P(("groups", "tok"), ("head", "sub"), None),
        P("groups"),
        P("groups"),
        P(("head", "sub"), None, None),
        P(("head", "sub"), None, None),
        P(("groups", "tok"), "head", "sub", None),
        P(("groups", "tok"), "head", "sub", None),
        P(("groups", "tok")),
        P(("groups", "tok"), "head"),
    )
    out_specs = (
        P(("groups", "tok"), ("head", "sub"), None),
        P(("groups", "tok"), "head", "sub", None),
    )
    sizes = (mesh.shape["tok"], mesh.shape["head"], mesh.shape["sub"])
    return jax.shard_map(
        functools.partial(local, sizes),
        mesh=mesh,
        in_specs=in_specs,
        out_specs=out_specs,
        check_vma=False,
    )
```

```python
import functools
import math

import jax
import jax.numpy as jnp
from jax import lax
from jax.experimental import pallas as pl
from jax.experimental.pallas import tpu as pltpu
from jax.sharding import PartitionSpec as P

C = 512
R = 64
DN = 128
DV = 128
TOK_BLOCK = 64
MOST_BLOCKS = 16
PAGE = 32

MASKED_SCORE = -1e30
LOG2E = math.log2(math.e)

VMEM_LIMIT = 46 * 1024 * 1024
KEY_CHUNK = 256
HEAD_GROUP = 4
HEAD_BLOCK = 16


def prompt_kernel(n_pieces, tok_ref, place_ref, blocks_ref, pad_ref, q_ref, wk_ref, wv_ref, *refs):
    pieces, (o_ref, keys_ref, k_scr, v_scr, s_scr, bias_scr, live_scr, out_scr) = refs[:n_pieces], refs[n_pieces:]
    key_chunk = KEY_CHUNK
    group, width, nq = q_ref.shape
    nk = keys_ref.shape[0]
    n_span = blocks_ref.shape[0]
    steps = o_ref.shape[1] // group
    origin = tok_ref[0] * nq - (nk - nq)
    scale = LOG2E / math.sqrt(DN + R)
    step = pl.program_id(0)

    starts, limits = [], []
    end = -origin
    for i in range(n_span):
        starts.append(end)
        end = end + blocks_ref[i] * TOK_BLOCK
        limits.append(end - pad_ref[i])

    def span_of(position):
        first, limit = starts[0], limits[0]
        for i in range(1, n_span):
            inside = position >= starts[i]
            first = jnp.where(inside, starts[i], first)
            limit = jnp.where(inside, limits[i], limit)
        return first, limit

    @pl.when(step == 0)
    def _():
        position = (nk - nq) + lax.broadcasted_iota(jnp.int32, (8, nq), 1)
        first, limit = span_of(position)
        final = jnp.minimum(position, limit - 1)
        live_scr[...] = (position < limit).astype(jnp.float32)
        def fill(i, _):
            key = i * 64 + lax.broadcasted_iota(jnp.int32, (64, nq), 0)
            visible = (key >= first[:1]) & (key <= final[:1])
            bias_scr[pl.ds(pl.multiple_of(i * 64, 64), 64), :] = jnp.where(visible, 0.0, MASKED_SCORE)
            return 0
        lax.fori_loop(0, nk // 64, fill, 0)
        for i, piece in enumerate(pieces):
            rows = pl.ds(pl.multiple_of(place_ref[i], 16), piece.shape[0])
            keys_ref[rows, :] = piece[:, :C]
            for g in range(group):
                k_scr[g, rows, DN:] = piece[:, C:]

    c_first = lax.div(span_of(jnp.int32(nk - nq))[0], key_chunk)

    def run(first):
        rows = slice(first, nk)

        def expand(g):
            weight = jnp.concatenate([wk_ref[g], wv_ref[g]], axis=1)
            both = jnp.dot(keys_ref[rows, :], weight, preferred_element_type=jnp.float32)
            both = both.astype(jnp.bfloat16)
            k_scr[g, rows, :DN] = both[:, :DN]
            v_scr[g, :, rows] = both[:, DN:].T

        def score(g):
            s = jnp.dot(k_scr[g, rows, :], q_ref[g], preferred_element_type=jnp.float32)
            s = s + bias_scr[rows, :]
            s_scr[g % 2, rows, :] = s
            return jnp.max(s, axis=0, keepdims=True) * scale

        def blend(g, top):
            p = jnp.exp2(s_scr[g % 2, rows, :] * scale - top)
            total = jnp.sum(p, axis=0, keepdims=True)
            out = jnp.dot(
                v_scr[g, :, rows], p.astype(jnp.bfloat16), preferred_element_type=jnp.float32
            )
            out = out * (live_scr[:1, :] / total)
            slot = lax.rem(step, steps) * group + g
            out_scr[slot, :nq, :] = out.T

        for g in range(min(2, group)):
            expand(g)
        top = score(0)
        for g in range(group):
            after = score(g + 1) if g + 1 < group else None
            if g + 2 < group:
                expand(g + 2)
            blend(g, top)
            top = after

    for c in range((nk - nq) // key_chunk + 1):
        @pl.when(c_first == c)
        def _(c=c):
            run(c * key_chunk)

    @pl.when(lax.rem(step, steps) == steps - 1)
    def _():
        heads = o_ref.shape[1]
        stride = out_scr.shape[1]
        flat = out_scr.reshape((heads + 1) * stride, DV)
        def move(i, _):
            for u in range(16):
                p = i * 16 + u
                o_ref[p] = flat[pl.ds(p, heads, stride=stride), :].astype(o_ref.dtype)
            return 0
        lax.fori_loop(0, nq // 16, move, 0)


def prompt_attention(tok, places, span_blocks, span_pad, queries, key_weight, value_weight, pieces):
    heads, width, nq = queries.shape
    nk = sum(piece.shape[0] for piece in pieces)
    group = math.gcd(HEAD_GROUP, heads)
    block = math.gcd(HEAD_BLOCK, heads)
    grid_spec = pltpu.PrefetchScalarGridSpec(
        num_scalar_prefetch=4,
        grid=(heads // group,),
        in_specs=[
            pl.BlockSpec((group, width, nq), lambda i, *_: (i, 0, 0)),
            pl.BlockSpec((group, C, DN), lambda i, *_: (i, 0, 0)),
            pl.BlockSpec((group, C, DV), lambda i, *_: (i, 0, 0)),
        ]
        + [pl.BlockSpec(piece.shape, lambda i, *_: (0, 0)) for piece in pieces],
        out_specs=pl.BlockSpec((nq, block, DV), lambda i, *_: (0, i // (block // group), 0)),
        scratch_shapes=[
            pltpu.VMEM((nk, C), jnp.bfloat16),
            pltpu.VMEM((group, nk, width), jnp.bfloat16),
            pltpu.VMEM((group, DV, nk), jnp.bfloat16),
            pltpu.VMEM((2, nk, nq), jnp.float32),
            pltpu.VMEM((nk, nq), jnp.float32),
            pltpu.VMEM((8, nq), jnp.float32),
            pltpu.VMEM((block + 1, nq + 8, DV), jnp.float32),
        ],
    )
    return pl.pallas_call(
        functools.partial(prompt_kernel, len(pieces)),
        out_shape=jax.ShapeDtypeStruct((nq, heads, DV), jnp.bfloat16),
        grid_spec=grid_spec,
        compiler_params=pltpu.CompilerParams(
            dimension_semantics=("arbitrary",), vmem_limit_bytes=VMEM_LIMIT
        ),
        cost_estimate=pl.CostEstimate(
            flops=2 * heads * nk * (C * (DN + DV) + nq * (width + DV)),
            bytes_accessed=24 << 20,
            transcendentals=heads * nq * nk,
        ),
        name="prompt_attention",
    )(tok, places, span_blocks, span_pad, queries, key_weight, value_weight, *pieces)


def decode_kernel(lengths_ref, pages_ref, other_pages_ref, qm_ref, qs_ref, mm_ref, ms_ref, om_ref, os_ref, o_ref):
    rows, width, slots = mm_ref.shape
    half = o_ref.shape[2]
    scale = LOG2E / math.sqrt(DN + R)
    lane = lax.broadcasted_iota(jnp.int32, (1, slots), 1)
    page_of, inside = lax.div(lane, PAGE), lax.rem(lane, PAGE)

    def ahead(ref, row):
        position = inside + ref[0, row] * PAGE
        for j in range(1, ref.shape[0]):
            position = jnp.where(page_of == j, inside + ref[j, row] * PAGE, position)
        return position - lengths_ref[row]

    def dot(a, b):
        return jnp.dot(a, b, preferred_element_type=jnp.float32)

    def blend(w, cache):
        return lax.dot_general(
            w.astype(jnp.bfloat16),
            cache,
            (((1,), (1,)), ((), ())),
            preferred_element_type=jnp.float32,
        )

    for row in range(rows):
        mine = jnp.concatenate([mm_ref[row], om_ref[row]], axis=1)
        paired = jnp.concatenate([ms_ref[row], os_ref[row]], axis=1)
        visible = jnp.concatenate([ahead(pages_ref, row), ahead(other_pages_ref, row)], axis=1) < 0
        s = dot(qm_ref[row], mine) + dot(qs_ref[row], paired)
        s = jnp.where(visible, s, MASKED_SCORE)
        top = jnp.max(s, axis=1, keepdims=True) * scale
        w = jnp.exp2(s * scale - top)
        total = jnp.sum(w, axis=1, keepdims=True)
        context = blend(w, mine[:half])
        o_ref[row] = (context / total).astype(o_ref.dtype)


def decode_pair(lengths, pages, other_pages, qm, qs, mm, ms, om, os):
    rows, heads, width = qm.shape
    half = width - R // 2
    smem = pl.BlockSpec(memory_space=pltpu.SMEM)
    vmem = pl.BlockSpec(memory_space=pltpu.VMEM)
    return pl.pallas_call(
        decode_kernel,
        out_shape=jax.ShapeDtypeStruct((rows, heads, half), jnp.bfloat16),
        in_specs=[smem] * 3 + [vmem] * 6,
        out_specs=vmem,
        compiler_params=pltpu.CompilerParams(vmem_limit_bytes=16 * 1024 * 1024),
        cost_estimate=pl.CostEstimate(
            flops=8 * rows * heads * mm.shape[2] * (width + half // 2),
            bytes_accessed=4 << 20,
            transcendentals=2 * rows * heads * mm.shape[2],
        ),
        name="decode_pair",
    )(lengths, pages, other_pages, qm, qs, mm, ms, om, os)


def swap(x, axis):
    return lax.ppermute(x, axis, [(0, 1), (1, 0)])


def prompt_pieces(prefill_latent, prefill_rope, sizes):
    n_tok, n_head, n_sub = sizes
    rows = prefill_latent.shape[1]
    block_rows = rows * n_head * n_sub
    back = min(n_tok - 1, -(-(MOST_BLOCKS - 1) * TOK_BLOCK // block_rows))
    own = jnp.concatenate([prefill_latent[0], prefill_rope[0]], axis=1)
    blocks = [own] + [
        lax.ppermute(own, "tok", [(i, i + d) for i in range(n_tok - d)]) for d in range(1, back + 1)
    ]
    if n_head == 2 and n_sub == 2:
        head, sub = lax.axis_index("head"), lax.axis_index("sub")
        pieces, places = [], []
        for d, mine in enumerate(blocks):
            far = swap(mine, "head")
            for h, x in enumerate((mine, far)):
                for s, y in enumerate((x, swap(x, "sub"))):
                    pieces.append(y)
                    index = ((back - d) * n_head + (head ^ h)) * n_sub + (sub ^ s)
                    places.append(index * rows)
        return pieces, jnp.stack(places).astype(jnp.int32)
    keys = jnp.stack(blocks[::-1])
    keys = lax.all_gather(keys, ("head", "sub"), axis=1, tiled=True)
    return [keys.reshape(-1, C + R)], jnp.zeros((1,), jnp.int32)


def decode_exchange(decode_query, decode_cache, decode_lengths, decode_pages):
    score_scale = 1.0 / math.sqrt(DN + R)
    queries_all = lax.all_gather(decode_query, "head", axis=1, tiled=True)
    partial_value = jnp.einsum(
        "bhsc,btsc->bht", queries_all, decode_cache, preferred_element_type=jnp.float32
    )
    scores = lax.psum(partial_value, "sub") * score_scale
    page_count = decode_pages.shape[1]
    logical = (
        jnp.repeat(decode_pages, PAGE, axis=1) * PAGE
        + jnp.tile(jnp.arange(PAGE, dtype=jnp.int32), page_count)[None, :]
    )
    live_tokens = logical < decode_lengths[:, None]
    scores = jnp.where(live_tokens[:, None, :], scores, MASKED_SCORE)
    peak_here = jnp.max(scores, axis=2)
    weights = jnp.where(live_tokens[:, None, :], jnp.exp(scores - peak_here[:, :, None]), 0.0)
    totals = jnp.sum(weights, axis=2)
    latent_half = decode_cache.shape[3] - R // 2
    context = jnp.einsum(
        "bht,btsc->bhsc",
        weights.astype(jnp.bfloat16),
        decode_cache[:, :, :, :latent_half],
        preferred_element_type=jnp.float32,
    )
    peaks_in, totals_in, context_in = (
        lax.all_to_all(peak_here[None], "head", split_axis=2, concat_axis=0, tiled=True),
        lax.all_to_all(totals[None], "head", split_axis=2, concat_axis=0, tiled=True),
        lax.all_to_all(context[None], "head", split_axis=2, concat_axis=0, tiled=True),
    )
    row_peak = jnp.max(peaks_in, axis=0)
    factor = jnp.exp(peaks_in - row_peak[None])
    denominators = jnp.sum(totals_in * factor, axis=0)
    summed = jnp.sum(context_in * factor[:, :, :, None, None], axis=0)
    decode_context = (summed / denominators[:, :, None, None]).astype(jnp.bfloat16)
    return decode_context


def local(
    sizes,
    prefill_query,
    prefill_latent,
    prefill_rope,
    span_blocks,
    span_pad,
    key_weight,
    value_weight,
    decode_query,
    decode_cache,
    decode_lengths,
    decode_pages,
):
    n_head, n_sub = sizes[1:]
    tok = lax.axis_index("tok")
    paired = n_head == 2 and n_sub == 2
    pieces, places = prompt_pieces(prefill_latent, prefill_rope, sizes)
    if paired:
        qm = decode_query[:, :, 0, :]
        mm = jnp.transpose(decode_cache[:, :, 0, :], (0, 2, 1))
        qs, ms = swap(qm, "sub"), swap(mm, "sub")
        mm_out, ms_out, *pieces = lax.optimization_barrier((mm, ms, *pieces))
        om, os = swap(mm_out, "head"), swap(ms_out, "head")
        pages = jnp.transpose(decode_pages)
        other_pages = swap(pages, "head")

    prefill_out = prompt_attention(
        tok[None].astype(jnp.int32),
        places,
        span_blocks,
        span_pad,
        jnp.transpose(prefill_query, (1, 2, 0)),
        key_weight,
        value_weight,
        pieces,
    )
    if paired:
        prefill_out, om, os, other_pages = lax.optimization_barrier((prefill_out, om, os, other_pages))
        context = decode_pair(decode_lengths, pages, other_pages, qm, qs, mm, ms, om, os)
        decode_context = context[:, :, None, :]
    else:
        decode_context = decode_exchange(decode_query, decode_cache, decode_lengths, decode_pages)
    return (prefill_out, decode_context)


def solution(mesh):
    in_specs = (
        P(("groups", "tok"), ("head", "sub"), None),
        P(("groups", "tok"), ("head", "sub"), None),
        P(("groups", "tok"), ("head", "sub"), None),
        P("groups"),
        P("groups"),
        P(("head", "sub"), None, None),
        P(("head", "sub"), None, None),
        P(("groups", "tok"), "head", "sub", None),
        P(("groups", "tok"), "head", "sub", None),
        P(("groups", "tok")),
        P(("groups", "tok"), "head"),
    )
    out_specs = (
        P(("groups", "tok"), ("head", "sub"), None),
        P(("groups", "tok"), "head", "sub", None),
    )
    sizes = (mesh.shape["tok"], mesh.shape["head"], mesh.shape["sub"])
    return jax.shard_map(
        functools.partial(local, sizes),
        mesh=mesh,
        in_specs=in_specs,
        out_specs=out_specs,
        check_vma=False,
    )
```

```python
import functools
import math

import jax
import jax.numpy as jnp
from jax import lax
from jax.experimental import pallas as pl
from jax.experimental.pallas import tpu as pltpu
from jax.sharding import PartitionSpec as P

C = 512
R = 64
DN = 128
DV = 128
TOK_BLOCK = 64
MOST_BLOCKS = 16
PAGE = 32

MASKED_SCORE = -1e30
LOG2E = math.log2(math.e)

VMEM_LIMIT = 56 * 1024 * 1024
KEY_CHUNK = 256
HEAD_GROUP = 8
HEAD_BLOCK = 16


def prompt_kernel(n_pieces, tok_ref, place_ref, blocks_ref, pad_ref, q_ref, wk_ref, wv_ref, *refs):
    pieces, (o_ref, keys_ref, k_scr, v_scr, s_scr, bias_scr, live_scr, out_scr) = refs[:n_pieces], refs[n_pieces:]
    key_chunk = KEY_CHUNK
    group, width, nq = q_ref.shape
    nk = keys_ref.shape[0]
    n_span = blocks_ref.shape[0]
    steps = o_ref.shape[1] // group
    origin = tok_ref[0] * nq - (nk - nq)
    scale = LOG2E / math.sqrt(DN + R)
    step = pl.program_id(0)

    starts, limits = [], []
    end = -origin
    for i in range(n_span):
        starts.append(end)
        end = end + blocks_ref[i] * TOK_BLOCK
        limits.append(end - pad_ref[i])

    def span_of(position):
        first, limit = starts[0], limits[0]
        for i in range(1, n_span):
            inside = position >= starts[i]
            first = jnp.where(inside, starts[i], first)
            limit = jnp.where(inside, limits[i], limit)
        return first, limit

    @pl.when(step == 0)
    def _():
        position = (nk - nq) + lax.broadcasted_iota(jnp.int32, (8, nq), 1)
        first, limit = span_of(position)
        final = jnp.minimum(position, limit - 1)
        live_scr[...] = (position < limit).astype(jnp.float32)
        def fill(i, _):
            key = i * 64 + lax.broadcasted_iota(jnp.int32, (64, nq), 0)
            visible = (key >= first[:1]) & (key <= final[:1])
            bias_scr[pl.ds(pl.multiple_of(i * 64, 64), 64), :] = jnp.where(visible, 0.0, MASKED_SCORE)
            return 0
        lax.fori_loop(0, nk // 64, fill, 0)
        for i, piece in enumerate(pieces):
            n = piece.shape[0] * C // (C + R)
            rows = pl.ds(pl.multiple_of(place_ref[i], 16), n)
            keys_ref[rows, :] = piece[:n, :]
            rope = jnp.concatenate([piece[n:, c : c + n] for c in range(0, C, n)], axis=0).T
            for g in range(group):
                k_scr[g, rows, DN:] = rope

    c_first = lax.div(span_of(jnp.int32(nk - nq))[0], key_chunk)

    def run(first):
        rows = slice(first, nk)

        def expand(g):
            weight = jnp.concatenate([wk_ref[g], wv_ref[g]], axis=1)
            both = jnp.dot(keys_ref[rows, :], weight, preferred_element_type=jnp.float32)
            both = both.astype(jnp.bfloat16)
            k_scr[g, rows, :DN] = both[:, :DN]
            v_scr[g, :, rows] = both[:, DN:].T

        def score(g):
            s = jnp.dot(k_scr[g, rows, :], q_ref[g], preferred_element_type=jnp.float32)
            s = s + bias_scr[rows, :]
            s_scr[g % 2, rows, :] = s
            return jnp.max(s, axis=0, keepdims=True) * scale

        def blend(g, top):
            p = jnp.exp2(s_scr[g % 2, rows, :] * scale - top)
            total = jnp.sum(p, axis=0, keepdims=True)
            out = jnp.dot(
                v_scr[g, :, rows], p.astype(jnp.bfloat16), preferred_element_type=jnp.float32
            )
            out = out * (live_scr[:1, :] / total)
            slot = lax.rem(step, steps) * group + g
            out_scr[slot, :nq, :] = out.T

        for g in range(min(2, group)):
            expand(g)
        top = score(0)
        for g in range(group):
            after = score(g + 1) if g + 1 < group else None
            if g + 2 < group:
                expand(g + 2)
            blend(g, top)
            top = after

    for c in range((nk - nq) // key_chunk + 1):
        @pl.when(c_first == c)
        def _(c=c):
            run(c * key_chunk)

    @pl.when(lax.rem(step, steps) == steps - 1)
    def _():
        heads = o_ref.shape[1]
        stride = out_scr.shape[1]
        flat = out_scr.reshape((heads + 1) * stride, DV)
        def move(i, _):
            for u in range(16):
                p = i * 16 + u
                o_ref[p] = flat[pl.ds(p, heads, stride=stride), :].astype(o_ref.dtype)
            return 0
        lax.fori_loop(0, nq // 16, move, 0)


def prompt_attention(tok, places, span_blocks, span_pad, queries, key_weight, value_weight, pieces):
    heads, width, nq = queries.shape
    nk = sum(piece.shape[0] for piece in pieces) * C // (C + R)
    group = math.gcd(HEAD_GROUP, heads)
    block = math.gcd(HEAD_BLOCK, heads)
    grid_spec = pltpu.PrefetchScalarGridSpec(
        num_scalar_prefetch=4,
        grid=(heads // group,),
        in_specs=[
            pl.BlockSpec((group, width, nq), lambda i, *_: (i, 0, 0)),
            pl.BlockSpec((group, C, DN), lambda i, *_: (i, 0, 0)),
            pl.BlockSpec((group, C, DV), lambda i, *_: (i, 0, 0)),
        ]
        + [pl.BlockSpec(piece.shape, lambda i, *_: (0, 0)) for piece in pieces],
        out_specs=pl.BlockSpec((nq, block, DV), lambda i, *_: (0, i // (block // group), 0)),
        scratch_shapes=[
            pltpu.VMEM((nk, C), jnp.bfloat16),
            pltpu.VMEM((group, nk, width), jnp.bfloat16),
            pltpu.VMEM((group, DV, nk), jnp.bfloat16),
            pltpu.VMEM((2, nk, nq), jnp.float32),
            pltpu.VMEM((nk, nq), jnp.float32),
            pltpu.VMEM((8, nq), jnp.float32),
            pltpu.VMEM((block + 1, nq + 8, DV), jnp.float32),
        ],
    )
    return pl.pallas_call(
        functools.partial(prompt_kernel, len(pieces)),
        out_shape=jax.ShapeDtypeStruct((nq, heads, DV), jnp.bfloat16),
        grid_spec=grid_spec,
        compiler_params=pltpu.CompilerParams(
            dimension_semantics=("arbitrary",), vmem_limit_bytes=VMEM_LIMIT
        ),
        cost_estimate=pl.CostEstimate(
            flops=2 * heads * nk * (C * (DN + DV) + nq * (width + DV)),
            bytes_accessed=24 << 20,
            transcendentals=heads * nq * nk,
        ),
        name="prompt_attention",
    )(tok, places, span_blocks, span_pad, queries, key_weight, value_weight, *pieces)


def decode_kernel(lengths_ref, qm_ref, qs_ref, mm_ref, ms_ref, om_ref, os_ref, o_ref):
    rows, width, _ = ms_ref.shape
    half = o_ref.shape[2]
    scale = LOG2E / math.sqrt(DN + R)
    first = pl.program_id(0) * rows

    def dot(a, b):
        return jnp.dot(a, b, preferred_element_type=jnp.float32)

    for row in range(rows):
        mine = jnp.concatenate([mm_ref[row], om_ref[row]], axis=1)
        paired = jnp.concatenate([ms_ref[row], os_ref[row]], axis=1)
        position = mine[width:].astype(jnp.float32)[:1].astype(jnp.int32)
        s = dot(qm_ref[row], mine[:width]) + dot(qs_ref[row], paired)
        s = jnp.where(position < lengths_ref[first + row], s, MASKED_SCORE)
        top = jnp.max(s, axis=1, keepdims=True) * scale
        w = jnp.exp2(s * scale - top)
        total = jnp.sum(w, axis=1, keepdims=True)
        context = lax.dot_general(
            w.astype(jnp.bfloat16),
            mine[:half],
            (((1,), (1,)), ((), ())),
            preferred_element_type=jnp.float32,
        )
        o_ref[row] = (context / total).astype(o_ref.dtype)


def decode_pair(lengths, qm, qs, mm, ms, om, os):
    rows, heads, width = qm.shape
    half = width - R // 2
    step = math.gcd(2, rows)

    def block(x):
        return pl.BlockSpec((step,) + x.shape[1:], lambda i: (i, 0, 0))

    return pl.pallas_call(
        decode_kernel,
        out_shape=jax.ShapeDtypeStruct((rows, heads, half), jnp.bfloat16),
        grid=(rows // step,),
        in_specs=[pl.BlockSpec(memory_space=pltpu.SMEM)]
        + [block(x) for x in (qm, qs, mm, ms, om, os)],
        out_specs=pl.BlockSpec((step, heads, half), lambda i: (i, 0, 0)),
        compiler_params=pltpu.CompilerParams(
            dimension_semantics=("arbitrary",), vmem_limit_bytes=16 * 1024 * 1024
        ),
        cost_estimate=pl.CostEstimate(
            flops=8 * rows * heads * mm.shape[2] * (width + half // 2),
            bytes_accessed=4 << 20,
            transcendentals=2 * rows * heads * mm.shape[2],
        ),
        name="decode_pair",
    )(lengths, qm, qs, mm, ms, om, os)


def swap(x, axis):
    return lax.ppermute(x, axis, [(0, 1), (1, 0)])


def pack_rows(latent, rope):
    n = latent.shape[0]
    parts = rope.T.reshape(C // n, R * n // C, n)
    return jnp.concatenate([latent, jnp.concatenate(list(parts), axis=1)], axis=0)


def prompt_pieces(prefill_latent, prefill_rope, sizes):
    n_tok, n_head, n_sub = sizes
    rows = prefill_latent.shape[1]
    block_rows = rows * n_head * n_sub
    back = min(n_tok - 1, -(-(MOST_BLOCKS - 1) * TOK_BLOCK // block_rows))
    paired = n_head == 2 and n_sub == 2
    if paired:
        own = pack_rows(prefill_latent[0], prefill_rope[0])
    else:
        own = jnp.concatenate([prefill_latent[0], prefill_rope[0]], axis=1)
    blocks = [own] + [
        lax.ppermute(own, "tok", [(i, i + d) for i in range(n_tok - d)]) for d in range(1, back + 1)
    ]
    if paired:
        head, sub = lax.axis_index("head"), lax.axis_index("sub")
        pieces, places = [], []
        for d, mine in enumerate(blocks):
            far = swap(mine, "head")
            for h, x in enumerate((mine, far)):
                for s, y in enumerate((x, swap(x, "sub"))):
                    pieces.append(y)
                    index = ((back - d) * n_head + (head ^ h)) * n_sub + (sub ^ s)
                    places.append(index * rows)
        return pieces, jnp.stack(places).astype(jnp.int32)
    keys = jnp.stack(blocks[::-1])
    keys = lax.all_gather(keys, ("head", "sub"), axis=1, tiled=True)
    keys = keys.reshape(-1, 128, C + R)
    pieces = [pack_rows(x[:, :C], x[:, C:]) for x in keys]
    return pieces, 128 * jnp.arange(len(pieces), dtype=jnp.int32)


def decode_exchange(decode_query, decode_cache, decode_lengths, decode_pages):
    score_scale = 1.0 / math.sqrt(DN + R)
    queries_all = lax.all_gather(decode_query, "head", axis=1, tiled=True)
    partial_value = jnp.einsum(
        "bhsc,btsc->bht", queries_all, decode_cache, preferred_element_type=jnp.float32
    )
    scores = lax.psum(partial_value, "sub") * score_scale
    page_count = decode_pages.shape[1]
    logical = (
        jnp.repeat(decode_pages, PAGE, axis=1) * PAGE
        + jnp.tile(jnp.arange(PAGE, dtype=jnp.int32), page_count)[None, :]
    )
    live_tokens = logical < decode_lengths[:, None]
    scores = jnp.where(live_tokens[:, None, :], scores, MASKED_SCORE)
    peak_here = jnp.max(scores, axis=2)
    weights = jnp.where(live_tokens[:, None, :], jnp.exp(scores - peak_here[:, :, None]), 0.0)
    totals = jnp.sum(weights, axis=2)
    latent_half = decode_cache.shape[3] - R // 2
    context = jnp.einsum(
        "bht,btsc->bhsc",
        weights.astype(jnp.bfloat16),
        decode_cache[:, :, :, :latent_half],
        preferred_element_type=jnp.float32,
    )
    peaks_in, totals_in, context_in = (
        lax.all_to_all(peak_here[None], "head", split_axis=2, concat_axis=0, tiled=True),
        lax.all_to_all(totals[None], "head", split_axis=2, concat_axis=0, tiled=True),
        lax.all_to_all(context[None], "head", split_axis=2, concat_axis=0, tiled=True),
    )
    row_peak = jnp.max(peaks_in, axis=0)
    factor = jnp.exp(peaks_in - row_peak[None])
    denominators = jnp.sum(totals_in * factor, axis=0)
    summed = jnp.sum(context_in * factor[:, :, :, None, None], axis=0)
    decode_context = (summed / denominators[:, :, None, None]).astype(jnp.bfloat16)
    return decode_context


def local(
    sizes,
    prefill_query,
    prefill_latent,
    prefill_rope,
    span_blocks,
    span_pad,
    key_weight,
    value_weight,
    decode_query,
    decode_cache,
    decode_lengths,
    decode_pages,
):
    n_head, n_sub = sizes[1:]
    tok = lax.axis_index("tok")
    rows, slots = decode_cache.shape[:2]
    paired = n_head == 2 and n_sub == 2 and n_head * slots <= 256
    pieces, places = prompt_pieces(prefill_latent, prefill_rope, sizes)
    if paired:
        qm = decode_query[:, :, 0, :]
        cache = jnp.transpose(decode_cache[:, :, 0, :], (0, 2, 1))
        position = jnp.repeat(decode_pages * PAGE, PAGE, axis=1)
        position = position + (jnp.arange(slots, dtype=jnp.int32) % PAGE)[None, :]
        position = jnp.broadcast_to(position[:, None, :], (rows, 16, slots)).astype(cache.dtype)
        mm = jnp.concatenate([cache, position], axis=1)
        qs, ms = swap(qm, "sub"), swap(cache, "sub")
        mm_out, ms_out, *pieces = lax.optimization_barrier((mm, ms, *pieces))
        om, os = swap(mm_out, "head"), swap(ms_out, "head")

    prefill_out = prompt_attention(
        tok[None].astype(jnp.int32),
        places,
        span_blocks,
        span_pad,
        jnp.transpose(prefill_query, (1, 2, 0)),
        key_weight,
        value_weight,
        pieces,
    )
    if paired:
        prefill_out, om, os = lax.optimization_barrier((prefill_out, om, os))
        context = decode_pair(decode_lengths, qm, qs, mm, ms, om, os)
        decode_context = context[:, :, None, :]
    else:
        decode_context = decode_exchange(decode_query, decode_cache, decode_lengths, decode_pages)
    return (prefill_out, decode_context)


def solution(mesh):
    in_specs = (
        P(("groups", "tok"), ("head", "sub"), None),
        P(("groups", "tok"), ("head", "sub"), None),
        P(("groups", "tok"), ("head", "sub"), None),
        P("groups"),
        P("groups"),
        P(("head", "sub"), None, None),
        P(("head", "sub"), None, None),
        P(("groups", "tok"), "head", "sub", None),
        P(("groups", "tok"), "head", "sub", None),
        P(("groups", "tok")),
        P(("groups", "tok"), "head"),
    )
    out_specs = (
        P(("groups", "tok"), ("head", "sub"), None),
        P(("groups", "tok"), "head", "sub", None),
    )
    sizes = (mesh.shape["tok"], mesh.shape["head"], mesh.shape["sub"])
    return jax.shard_map(
        functools.partial(local, sizes),
        mesh=mesh,
        in_specs=in_specs,
        out_specs=out_specs,
        check_vma=False,
    )
```

```python
import functools
import math

import jax
import jax.numpy as jnp
import numpy as np
from jax import lax
from jax.experimental import pallas as pl
from jax.experimental.pallas import tpu as pltpu
from jax.sharding import PartitionSpec as P

C = 512
R = 64
DN = 128
DV = 128
TOK_BLOCK = 64
MOST_BLOCKS = 16
PAGE = 32

MASKED_SCORE = -1e30
LOG2E = math.log2(math.e)

VMEM_LIMIT = 56 * 1024 * 1024
KEY_CHUNK = 256
HEAD_GROUP = 4
HEAD_BLOCK = 16


def prompt_kernel(n_pieces, tok_ref, place_ref, blocks_ref, pad_ref, q_ref, wk_ref, wv_ref, *refs):
    pieces, (o_ref, keys_ref, k_scr, v_scr, s_scr, bias_scr, live_scr, out_scr) = refs[:n_pieces], refs[n_pieces:]
    key_chunk = KEY_CHUNK
    group, width, nq = q_ref.shape
    nk = keys_ref.shape[0]
    n_span = blocks_ref.shape[0]
    steps = o_ref.shape[1] // group
    origin = tok_ref[0] * nq - (nk - nq)
    scale = LOG2E / math.sqrt(DN + R)
    step = pl.program_id(0)

    starts, limits = [], []
    end = -origin
    for i in range(n_span):
        starts.append(end)
        end = end + blocks_ref[i] * TOK_BLOCK
        limits.append(end - pad_ref[i])

    def span_of(position):
        first, limit = starts[0], limits[0]
        for i in range(1, n_span):
            inside = position >= starts[i]
            first = jnp.where(inside, starts[i], first)
            limit = jnp.where(inside, limits[i], limit)
        return first, limit

    @pl.when(step == 0)
    def _():
        position = (nk - nq) + lax.broadcasted_iota(jnp.int32, (8, nq), 1)
        first, limit = span_of(position)
        final = jnp.minimum(position, limit - 1)
        live_scr[...] = (position < limit).astype(jnp.float32)
        def fill(i, _):
            key = i * 64 + lax.broadcasted_iota(jnp.int32, (64, nq), 0)
            visible = (key >= first[:1]) & (key <= final[:1])
            bias_scr[pl.ds(pl.multiple_of(i * 64, 64), 64), :] = jnp.where(visible, 0.0, MASKED_SCORE)
            return 0
        lax.fori_loop(0, nk // 64, fill, 0)
        for i, piece in enumerate(pieces):
            n = piece.shape[0] * C // (C + R)
            rows = pl.ds(pl.multiple_of(place_ref[i], 16), n)
            keys_ref[rows, :] = piece[:n, :]
            rope = jnp.concatenate([piece[n:, c : c + n] for c in range(0, C, n)], axis=0).T
            for g in range(group):
                k_scr[g, rows, DN:] = rope

    c_first = lax.div(span_of(jnp.int32(nk - nq))[0], key_chunk)

    def run(first):
        rows = slice(first, nk)

        def expand(g):
            weight = jnp.concatenate([wk_ref[g], wv_ref[g]], axis=1)
            both = jnp.dot(keys_ref[rows, :], weight, preferred_element_type=jnp.float32)
            both = both.astype(jnp.bfloat16)
            k_scr[g, rows, :DN] = both[:, :DN]
            v_scr[g, :, rows] = both[:, DN:].T

        def score(g):
            s = jnp.dot(k_scr[g, rows, :], q_ref[g], preferred_element_type=jnp.float32)
            s = s + bias_scr[rows, :]
            s_scr[g % 2, rows, :] = s
            return jnp.max(s, axis=0, keepdims=True) * scale

        def blend(g, top):
            p = jnp.exp2(s_scr[g % 2, rows, :] * scale - top)
            total = jnp.sum(p, axis=0, keepdims=True)
            out = jnp.dot(
                v_scr[g, :, rows], p.astype(jnp.bfloat16), preferred_element_type=jnp.float32
            )
            out = out * (live_scr[:1, :] / total)
            slot = lax.rem(step, steps) * group + g
            out_scr[slot, :nq, :] = out.T

        for g in range(min(2, group)):
            expand(g)
        top = score(0)
        for g in range(group):
            after = score(g + 1) if g + 1 < group else None
            if g + 2 < group:
                expand(g + 2)
            blend(g, top)
            top = after

    for c in range((nk - nq) // key_chunk + 1):
        @pl.when(c_first == c)
        def _(c=c):
            run(c * key_chunk)

    @pl.when(lax.rem(step, steps) == steps - 1)
    def _():
        heads = o_ref.shape[1]
        stride = out_scr.shape[1]
        flat = out_scr.reshape((heads + 1) * stride, DV)
        def move(i, _):
            for u in range(16):
                p = i * 16 + u
                o_ref[p] = flat[pl.ds(p, heads, stride=stride), :].astype(o_ref.dtype)
            return 0
        lax.fori_loop(0, nq // 16, move, 0)


def prompt_attention(tok, places, span_blocks, span_pad, queries, key_weight, value_weight, pieces):
    heads, width, nq = queries.shape
    nk = sum(piece.shape[0] for piece in pieces) * C // (C + R)
    group = math.gcd(HEAD_GROUP, heads)
    block = math.gcd(HEAD_BLOCK, heads)
    grid_spec = pltpu.PrefetchScalarGridSpec(
        num_scalar_prefetch=4,
        grid=(heads // group,),
        in_specs=[
            pl.BlockSpec((group, width, nq), lambda i, *_: (i, 0, 0)),
            pl.BlockSpec((group, C, DN), lambda i, *_: (i, 0, 0)),
            pl.BlockSpec((group, C, DV), lambda i, *_: (i, 0, 0)),
        ]
        + [pl.BlockSpec(piece.shape, lambda i, *_: (0, 0)) for piece in pieces],
        out_specs=pl.BlockSpec((nq, block, DV), lambda i, *_: (0, i // (block // group), 0)),
        scratch_shapes=[
            pltpu.VMEM((nk, C), jnp.bfloat16),
            pltpu.VMEM((group, nk, width), jnp.bfloat16),
            pltpu.VMEM((group, DV, nk), jnp.bfloat16),
            pltpu.VMEM((2, nk, nq), jnp.float32),
            pltpu.VMEM((nk, nq), jnp.float32),
            pltpu.VMEM((8, nq), jnp.float32),
            pltpu.VMEM((block + 1, nq + 8, DV), jnp.float32),
        ],
    )
    return pl.pallas_call(
        functools.partial(prompt_kernel, len(pieces)),
        out_shape=jax.ShapeDtypeStruct((nq, heads, DV), jnp.bfloat16),
        grid_spec=grid_spec,
        compiler_params=pltpu.CompilerParams(
            dimension_semantics=("arbitrary",), vmem_limit_bytes=VMEM_LIMIT
        ),
        cost_estimate=pl.CostEstimate(
            flops=2 * heads * nk * (C * (DN + DV) + nq * (width + DV)),
            bytes_accessed=24 << 20,
            transcendentals=heads * nq * nk,
        ),
        name="prompt_attention",
    )(tok, places, span_blocks, span_pad, queries, key_weight, value_weight, *pieces)


def decode_kernel(lengths_ref, qm_ref, qs_ref, mm_ref, ms_ref, om_ref, os_ref, o_ref):
    rows, width, _ = ms_ref.shape
    half = o_ref.shape[2]
    scale = LOG2E / math.sqrt(DN + R)
    first = pl.program_id(0) * rows

    def dot(a, b):
        return jnp.dot(a, b, preferred_element_type=jnp.float32)

    for row in range(rows):
        mine = jnp.concatenate([mm_ref[row], om_ref[row]], axis=1)
        paired = jnp.concatenate([ms_ref[row], os_ref[row]], axis=1)
        position = mine[width:].astype(jnp.float32)[:1].astype(jnp.int32)
        s = dot(qm_ref[row], mine[:width]) + dot(qs_ref[row], paired)
        s = jnp.where(position < lengths_ref[first + row], s, MASKED_SCORE)
        top = jnp.max(s, axis=1, keepdims=True) * scale
        w = jnp.exp2(s * scale - top)
        total = jnp.sum(w, axis=1, keepdims=True)
        context = lax.dot_general(
            w.astype(jnp.bfloat16),
            mine[:half],
            (((1,), (1,)), ((), ())),
            preferred_element_type=jnp.float32,
        )
        o_ref[row] = (context / total).astype(o_ref.dtype)


def decode_pair(lengths, qm, qs, mm, ms, om, os):
    rows, heads, width = qm.shape
    half = width - R // 2
    step = math.gcd(2, rows)

    def block(x):
        return pl.BlockSpec((step,) + x.shape[1:], lambda i: (i, 0, 0))

    return pl.pallas_call(
        decode_kernel,
        out_shape=jax.ShapeDtypeStruct((rows, heads, half), jnp.bfloat16),
        grid=(rows // step,),
        in_specs=[pl.BlockSpec(memory_space=pltpu.SMEM)]
        + [block(x) for x in (qm, qs, mm, ms, om, os)],
        out_specs=pl.BlockSpec((step, heads, half), lambda i: (i, 0, 0)),
        compiler_params=pltpu.CompilerParams(
            dimension_semantics=("arbitrary",), vmem_limit_bytes=16 * 1024 * 1024
        ),
        cost_estimate=pl.CostEstimate(
            flops=8 * rows * heads * mm.shape[2] * (width + half // 2),
            bytes_accessed=4 << 20,
            transcendentals=2 * rows * heads * mm.shape[2],
        ),
        name="decode_pair",
    )(lengths, qm, qs, mm, ms, om, os)


def swap(x, axis):
    return lax.ppermute(x, axis, [(0, 1), (1, 0)])


def pack_rows(latent, rope):
    n = latent.shape[0]
    parts = rope.T.reshape(C // n, R * n // C, n)
    return jnp.concatenate([latent, jnp.concatenate(list(parts), axis=1)], axis=0)


def prompt_pieces(prefill_latent, prefill_rope, cache, sizes):
    n_tok, n_head, n_sub = sizes
    rows = prefill_latent.shape[1]
    block_rows = rows * n_head * n_sub
    back = min(n_tok - 1, -(-(MOST_BLOCKS - 1) * TOK_BLOCK // block_rows))
    paired = n_head == 2 and n_sub == 2
    if paired:
        own = pack_rows(prefill_latent[0], prefill_rope[0])
    else:
        own = jnp.concatenate([prefill_latent[0], prefill_rope[0]], axis=1)
    blocks = [own] + [
        lax.ppermute(own, "tok", [(i, i + d) for i in range(n_tok - d)]) for d in range(1, back + 1)
    ]
    if paired:
        head, sub = lax.axis_index("head"), lax.axis_index("sub")
        pieces = []
        for d, mine in enumerate(blocks):
            far = swap(mine, "head")
            if d == 0:
                far, cache = lax.optimization_barrier((far, cache))
            for x in (mine, far):
                pieces += [x, swap(x, "sub")]
        pair = np.arange(len(pieces), dtype=np.int32)
        block, pair = (back - pair // 4) * 4, pair % 4
        places = (block + (pair ^ (head * 2 + sub))) * rows
        return pieces, places.astype(jnp.int32), cache
    keys = jnp.stack(blocks[::-1])
    keys = lax.all_gather(keys, ("head", "sub"), axis=1, tiled=True)
    keys = keys.reshape(-1, 128, C + R)
    pieces = [pack_rows(x[:, :C], x[:, C:]) for x in keys]
    return pieces, 128 * jnp.arange(len(pieces), dtype=jnp.int32), cache


def decode_exchange(decode_query, decode_cache, decode_lengths, decode_pages):
    score_scale = 1.0 / math.sqrt(DN + R)
    queries_all = lax.all_gather(decode_query, "head", axis=1, tiled=True)
    partial_value = jnp.einsum(
        "bhsc,btsc->bht", queries_all, decode_cache, preferred_element_type=jnp.float32
    )
    scores = lax.psum(partial_value, "sub") * score_scale
    page_count = decode_pages.shape[1]
    logical = (
        jnp.repeat(decode_pages, PAGE, axis=1) * PAGE
        + jnp.tile(jnp.arange(PAGE, dtype=jnp.int32), page_count)[None, :]
    )
    live_tokens = logical < decode_lengths[:, None]
    scores = jnp.where(live_tokens[:, None, :], scores, MASKED_SCORE)
    peak_here = jnp.max(scores, axis=2)
    weights = jnp.where(live_tokens[:, None, :], jnp.exp(scores - peak_here[:, :, None]), 0.0)
    totals = jnp.sum(weights, axis=2)
    latent_half = decode_cache.shape[3] - R // 2
    context = jnp.einsum(
        "bht,btsc->bhsc",
        weights.astype(jnp.bfloat16),
        decode_cache[:, :, :, :latent_half],
        preferred_element_type=jnp.float32,
    )
    peaks_in, totals_in, context_in = (
        lax.all_to_all(peak_here[None], "head", split_axis=2, concat_axis=0, tiled=True),
        lax.all_to_all(totals[None], "head", split_axis=2, concat_axis=0, tiled=True),
        lax.all_to_all(context[None], "head", split_axis=2, concat_axis=0, tiled=True),
    )
    row_peak = jnp.max(peaks_in, axis=0)
    factor = jnp.exp(peaks_in - row_peak[None])
    denominators = jnp.sum(totals_in * factor, axis=0)
    summed = jnp.sum(context_in * factor[:, :, :, None, None], axis=0)
    decode_context = (summed / denominators[:, :, None, None]).astype(jnp.bfloat16)
    return decode_context


def local(
    sizes,
    prefill_query,
    prefill_latent,
    prefill_rope,
    span_blocks,
    span_pad,
    key_weight,
    value_weight,
    decode_query,
    decode_cache,
    decode_lengths,
    decode_pages,
):
    n_head, n_sub = sizes[1:]
    tok = lax.axis_index("tok")
    rows, slots = decode_cache.shape[:2]
    paired = n_head == 2 and n_sub == 2 and n_head * slots <= 256
    mm = decode_cache
    if paired:
        qm = decode_query[:, :, 0, :]
        cache = jnp.transpose(decode_cache[:, :, 0, :], (0, 2, 1))
        position = jnp.repeat(decode_pages * PAGE, PAGE, axis=1)
        position = position + (jnp.arange(slots, dtype=jnp.int32) % PAGE)[None, :]
        position = jnp.broadcast_to(position[:, None, :], (rows, 16, slots)).astype(cache.dtype)
        mm = jnp.concatenate([cache, position], axis=1)
    pieces, places, mm = prompt_pieces(prefill_latent, prefill_rope, mm, sizes)
    if paired:
        qs, ms = swap(qm, "sub"), swap(cache, "sub")
        mm_out, ms_out, *pieces = lax.optimization_barrier((mm, ms, *pieces))
        om, os = swap(mm_out, "head"), swap(ms_out, "head")

    prefill_out = prompt_attention(
        tok[None].astype(jnp.int32),
        places,
        span_blocks,
        span_pad,
        jnp.transpose(prefill_query, (1, 2, 0)),
        key_weight,
        value_weight,
        pieces,
    )
    if paired:
        prefill_out, om, os = lax.optimization_barrier((prefill_out, om, os))
        context = decode_pair(decode_lengths, qm, qs, mm, ms, om, os)
        decode_context = context[:, :, None, :]
    else:
        decode_context = decode_exchange(decode_query, decode_cache, decode_lengths, decode_pages)
    return (prefill_out, decode_context)


def solution(mesh):
    in_specs = (
        P(("groups", "tok"), ("head", "sub"), None),
        P(("groups", "tok"), ("head", "sub"), None),
        P(("groups", "tok"), ("head", "sub"), None),
        P("groups"),
        P("groups"),
        P(("head", "sub"), None, None),
        P(("head", "sub"), None, None),
        P(("groups", "tok"), "head", "sub", None),
        P(("groups", "tok"), "head", "sub", None),
        P(("groups", "tok")),
        P(("groups", "tok"), "head"),
    )
    out_specs = (
        P(("groups", "tok"), ("head", "sub"), None),
        P(("groups", "tok"), "head", "sub", None),
    )
    sizes = (mesh.shape["tok"], mesh.shape["head"], mesh.shape["sub"])
    return jax.shard_map(
        functools.partial(local, sizes),
        mesh=mesh,
        in_specs=in_specs,
        out_specs=out_specs,
        check_vma=False,
    )
```
